256 devices in a mesh: dp: 128 (over x_lo, z, y, core), mp: 2 (over x_hi).
Axes of the slice: x: 4 (x_hi: 2, x_lo: 2; x = x_hi * 2 + x_lo), y: 4, z: 8, core: 2. Of those that a mesh axis runs over, the one named last changes fastest.
Arguments:
- image_in: bfloat16 [16384, 1536], P('dp', 'mp'), may hold values from -24 to 24
- text_in: bfloat16 [16384, 1536], P('dp', 'mp'), may hold values from -24 to 24
- image_w: bfloat16 [1536, 1536], P('mp'), may hold values from -0.15625 to 0.15625
- text_w: bfloat16 [1536, 1536], P('mp'), may hold values from -0.15625 to 0.15625
- logit_scale: float32 [], replicated, may hold values from 5 to 15
- logit_bias: float32 [], replicated, may hold values from -5 to -2
Outputs:
- grad_image_in: bfloat16 [16384, 1536], P('dp', 'mp')
- grad_text_in: bfloat16 [16384, 1536], P('dp', 'mp')
- grad_image_w: float32 [1536, 1536], P(('mp', 'dp'))
- grad_text_w: float32 [1536, 1536], P(('mp', 'dp'))
The draws below stay inside these ranges and needn't reach their ends.
All inputs are finite; a program needn't handle non-finite values.
Results may differ from the reference program's by a relative error of at most 0.0075.
Values may be sent and summed in bfloat16 or wider, within the bound.
A program may use at most 64 MiB of HBM per device.

```python
import jax
import jax.numpy as jnp
from jax import lax

D = 1536
E = 1536
PAIRS_DEV = 128
STEPS = 16
PAIRS = 16384


def raised(drawn, key, source, target, parts, factor):
    owner, partner = [(jnp.arange(drawn.shape[axis_at]) // (drawn.shape[axis_at] // parts)).reshape([-1 if axis == axis_at else 1 for axis in range(drawn.ndim)]) for axis_at in (source, target)]
    chosen = jax.random.permutation(key, parts)[partner]
    strong = (owner == chosen) | (owner == (partner + parts // 2) % parts)
    return jnp.where(strong, factor * drawn, drawn)


def steps_of(key, dims, shards, least, top_value):
    def one(position, parts):
        heights = jax.random.uniform(jax.random.fold_in(jax.random.fold_in(key, 6), position), (parts,), jnp.float32, least / len(shards), top_value / len(shards))
        return jnp.repeat(jnp.exp(heights), dims[position] // parts).reshape((-1,) + (1,) * (len(dims) - position - 1))

    gain = one(*shards[0])
    for cut in shards[1:]:
        gain = gain * one(*cut)
    return gain


def centred(rng, dims, spread, reach, split=(), kind=jnp.bfloat16):
    entries = jax.random.normal(rng, dims, jnp.float32) * spread
    if len(split) > 0:
        entries = steps_of(rng, dims, split, -0.22, 0.18) * entries
    return jnp.clip(entries, min=-reach, max=reach).astype(kind)


def bell_draw_with(key, extent, spread, most, shards, heavy, kind=jnp.bfloat16):
    entries = spread * jax.random.normal(key, extent, jnp.float32)
    if shards:
        entries = entries * steps_of(key, extent, shards, -0.22, 0.18)
    return jnp.clip(raised(entries, jax.random.fold_in(key, 3), *heavy), -most, most).astype(kind)


def setup_inputs(seed: int = 0) -> dict:
    seeds = jax.random.split(jax.random.key(seed), 7)
    image_in = bell_draw_with(seeds[0], (PAIRS, D), 1.0, 24.0, ((0, 128), (1, 2)), (0, 1, 128, 5.5))
    text_in = bell_draw_with(seeds[1], (PAIRS, D), 1.0, 24.0, ((0, 128), (1, 2)), (0, 1, 128, 5.5))
    image_w = centred(seeds[2], (D, E), D ** -0.5, 0.15625, ((0, 2),))
    text_w = centred(seeds[3], (D, E), D ** -0.5, 0.15625, ((0, 2),))
    logit_scale = jnp.clip(jax.random.uniform(seeds[4], (), jnp.float32, 5.0, 15.0), 5.0, 15.0)
    logit_bias = jnp.clip(jax.random.uniform(seeds[5], (), jnp.float32, -5.0, -2.0), -5.0, -2.0)
    return dict(image_in=image_in, text_in=text_in, image_w=image_w, text_w=text_w, logit_scale=logit_scale, logit_bias=logit_bias)


def project(features, weight):
    y = jnp.dot(features, weight, preferred_element_type=jnp.float32)
    inv_norm = jax.lax.rsqrt(lax.optimization_barrier(jnp.sum(y * y, axis=-1, keepdims=True)) + 1e-06)
    unit = y * inv_norm
    return (unit, inv_norm)

def backward(unit, inv_norm, upstream, features, weight):
    dy = (inv_norm * (upstream - unit * lax.optimization_barrier(jnp.sum(unit * upstream, axis=-1, keepdims=True)))).astype(jnp.bfloat16)
    grad_in = jnp.dot(dy, weight.T, preferred_element_type=jnp.float32).astype(jnp.bfloat16)
    grad_w = jnp.dot(features.T, dy, preferred_element_type=jnp.float32)
    return (grad_in, grad_w)

def reference(image_in, text_in, image_w, text_w, logit_scale, logit_bias):
    unit_i, norm_i = project(image_in, image_w)
    unit_t, norm_t = project(text_in, text_w)
    count = image_in.shape[0] // PAIRS_DEV
    blocks_i = unit_i.astype(jnp.bfloat16).reshape(count, PAIRS_DEV, E).astype(jnp.float32)
    blocks_t = unit_t.astype(jnp.bfloat16).reshape(count, PAIRS_DEV, E).astype(jnp.float32)
    total = float(PAIRS)
    eye = jnp.eye(PAIRS_DEV, dtype=jnp.float32)
    d_image = jnp.zeros((count, PAIRS_DEV, E), jnp.float32)
    d_text = jnp.zeros((count, PAIRS_DEV, E), jnp.float32)
    for step in range(STEPS):
        texts = jnp.roll(blocks_t, -step, 0)
        dots = jnp.einsum('kie,kje->kij', blocks_i, texts)
        logits = logit_scale * dots + logit_bias
        if step == 0:
            sign = 2.0 * eye - 1.0
        else:
            sign = -jnp.ones_like(eye)
        grad = -sign * jax.nn.sigmoid(-sign * logits) / total
        weighted = (logit_scale * grad).astype(jnp.bfloat16).astype(jnp.float32)
        d_image = d_image + jnp.einsum('kij,kje->kie', weighted, texts)
        d_text = d_text + jnp.roll(jnp.einsum('kij,kie->kje', weighted, blocks_i), step, 0)
    gx_i, gw_i = backward(unit_i, norm_i, d_image.reshape(-1, E), image_in, image_w)
    gx_t, gw_t = backward(unit_t, norm_t, d_text.reshape(-1, E), text_in, text_w)
    return (gx_i, gx_t, gw_i, gw_t)
```

```python
import jax
import jax.numpy as jnp
from jax import lax
from jax.experimental import pallas as pl
from jax.experimental.pallas import tpu as pltpu
from jax.sharding import PartitionSpec as P

MESH = pl.DeviceIdType.MESH
F32, BF16 = jnp.float32, jnp.bfloat16
ROWS = 128
HALF = 768
E = 1536
NY, NZ = 4, 8
SLICE = E // NY
STEPS = 16
SLOTS = 9
NCH = 2
CH = ROWS // NCH
PAIRS = 16384.0


def contract(a, b, da, db):
    return lax.dot_general(a, b, (((da,), (db,)), ((), ())), preferred_element_type=F32)


def body(
    image_in, text_in, image_w, text_w, scale_ref, bias_ref,
    gxi_ref, gxt_ref, gwi_ref, gwt_ref,
    x, w, part, px_send, px_recv, buf, own, y_own, inv_own, weights, acc, d_recv,
    dy, dy_slices, dy_other, gx, xg, dyg, g_send, xr, z_send, zr, f_send, f_recv,
    ld_sem, xg_ss, xg_rs, px_ss, px_rs, zs_ss, ys_ss, bf_rs, ow_ss, ow_rs, d_ss, d_rs,
    x2_ss, x2_rs, dg_ss, dg_rs, xr_ss, xr_rs, z_ss, z_rs, f_ss, f_rs,
):
    dp, r = lax.axis_index("dp"), lax.axis_index("mp")
    h, y, z, xl = dp % 2, (dp // 2) % NY, (dp // 8) % NZ, dp // 64
    m = dp + r * (127 - 2 * dp)
    hh, my, plane = m % 2, (m // 2) % NY, m // 8

    def at(xl_, z_, y_, core, mp):
        return (((xl_ * NZ + z_) * NY + y_) * 2 + core, mp)

    def mirrored(m_):
        return (m_ + r * (127 - 2 * m_), r)

    sibling = at(xl, z, y, 1 - h, r)
    partner = at(xl, z, y, h, 1 - r)
    across = at(1 - xl, z, y, r, h)

    pending = []

    def send(src, dst, ss, rs, device, when=None):
        def copy():
            return pltpu.make_async_remote_copy(
                src_ref=src, dst_ref=dst, send_sem=ss, recv_sem=rs, device_id=device, device_id_type=MESH
            )

        if when is None:
            copy().start()
            pending.append(lambda: copy().wait_send())
        else:

            @pl.when(when)
            def _():
                copy().start()

            def finish():
                @pl.when(when)
                def _():
                    copy().wait_send()

            pending.append(finish)

    def arrived(dst, rs):
        pltpu.make_async_copy(dst, dst, rs).wait()

    def load(src, dst, i):
        copy = pltpu.make_async_copy(src, dst, ld_sem.at[i])
        copy.start()
        return copy

    loads = [
        load(image_in, x.at[0], 0),
        load(text_in, x.at[1], 1),
        load(image_w, w.at[0], 2),
        load(text_w, w.at[1], 3),
    ]
    bar = pltpu.get_barrier_semaphore()
    peers = [sibling, partner, at(xl, z, y, 1 - h, 1 - r), across]
    peers += [at(xl, z, (y + d) % NY, c, r) for d in range(1, NY) for c in (0, 1)]
    peers += [at(xl, (z + d) % NZ, y, h, r) for d in range(1, NZ)]
    peers += [mirrored((m + 8) % 128), mirrored((m + 120) % 128)]
    for peer in peers:
        pl.semaphore_signal(bar, inc=1, device_id=peer, device_id_type=MESH)
    for copy in loads[:2]:
        copy.wait()
    pl.semaphore_wait(bar, len(peers))

    mine = 2 * y + h
    send(x.at[1 - r], xg.at[mine], xg_ss.at[0], xg_rs.at[mine], at(xl, z, y, r, 1 - r))
    for d in range(1, NY):
        send(x.at[r], xg.at[mine], xg_ss.at[d], xg_rs.at[mine], at(xl, z, (y + d) % NY, r, r))
    send(x.at[r], xg.at[mine], xg_ss.at[4], xg_rs.at[mine], sibling, hh == 1)

    @pl.when(hh == 0)
    def _():
        pltpu.make_async_copy(x.at[r], xg.at[mine], xg_rs.at[mine]).start()

    for copy in loads[2:]:
        copy.wait()
    for k, tower in ((0, r), (1, 1 - r)):
        features = x[tower]

        def column(i, c, k=k, tower=tower, features=features):
            cols = pl.ds(pl.multiple_of(i * 256, 256), 256)
            p = jnp.dot(features, w[tower, :, cols], preferred_element_type=F32)
            part[k, :, cols] = p
            px_send[k, :, cols] = p.astype(BF16)
            return c

        lax.fori_loop(0, E // 256, column, 0)
        for c in range(NCH):
            rows = pl.ds(c * CH, CH)
            send(px_send.at[k, rows], px_recv.at[k, rows], px_ss.at[k, c], px_rs.at[k, c], partner)

    for c in range(2):
        slot = 2 * y + c

        @pl.when(hh == 1)
        def _():
            arrived(xg.at[slot], xg_rs.at[slot])

        for d in range(1, NY):
            send(
                xg.at[slot], xg.at[slot], xg_ss.at[4 + 3 * c + d], xg_rs.at[slot],
                at(xl, z, (y + d) % NY, h, r), hh == 1,
            )

    def slot_rows(j, c):
        return pl.ds(pl.multiple_of(j * ROWS + c * CH, CH), CH)

    def y_peer(d):
        return mirrored(plane * 8 + ((my + d) % NY) * 2 + hh)

    z_peer = mirrored((m + 120) % 128)

    for c in range(NCH):
        rows = pl.ds(c * CH, CH)
        arrived(px_recv.at[0, rows], px_rs.at[0, c])
        yy = part[1, rows, :] + px_recv[0, rows, :].astype(F32)
        inv = lax.rsqrt(jnp.sum(yy * yy, axis=-1, keepdims=True) + 1e-06)
        buf[slot_rows(0, c), :] = (yy * inv).astype(BF16)
        src = buf.at[slot_rows(0, c)]
        send(src, buf.at[slot_rows(4, c)], zs_ss.at[0, c], bf_rs.at[4, c], z_peer)
        for d in range(1, NY):
            send(
                src, buf.at[slot_rows(4 - d, c)], ys_ss.at[0, d - 1, c], bf_rs.at[4 - d, c],
                y_peer(d), my + d >= NY,
            )
    for c in range(NCH):
        src = buf.at[slot_rows(4, c)]
        arrived(src, bf_rs.at[4, c])
        send(src, buf.at[slot_rows(8, c)], zs_ss.at[1, c], bf_rs.at[8, c], z_peer)
        for d in range(1, NY):
            slot = 4 - d + 4 * ((my + d) // NY)
            send(src, buf.at[slot_rows(slot, c)], ys_ss.at[1, d - 1, c], bf_rs.at[slot, c], y_peer(d))
    for c in range(NCH):
        rows = pl.ds(c * CH, CH)
        arrived(px_recv.at[1, rows], px_rs.at[1, c])
        yy = part[0, rows, :] + px_recv[1, rows, :].astype(F32)
        inv = lax.rsqrt(jnp.sum(yy * yy, axis=-1, keepdims=True) + 1e-06)
        unit = yy * inv
        y_own[rows, :] = unit
        inv_own[rows, :] = inv
        own[hh, rows, :] = unit.astype(BF16)
    send(own.at[hh], own.at[hh], ow_ss, ow_rs, sibling)
    for c in range(NCH):
        src = buf.at[slot_rows(8, c)]
        arrived(src, bf_rs.at[8, c])
        for d in range(1, NY):
            send(
                src, buf.at[slot_rows(8 - d, c)], ys_ss.at[2, d - 1, c], bf_rs.at[8 - d, c],
                y_peer(d), my + d < NY,
            )
    arrived(own.at[1 - hh], ow_rs)

    scale, bias = scale_ref[0, 0], bias_ref[0, 0]
    for j in (0, 4, 8, 3, 2, 1, 7, 6, 5):
        if j not in (0, 4, 8):
            for c in range(NCH):
                arrived(buf.at[slot_rows(j, c)], bf_rs.at[j, c])
        cols = pl.ds(j * ROWS, ROWS)
        for a in range(2):
            dots = contract(own[a], buf[cols, :], 1, 1)
            logits = scale * dots + bias
            if j == 0:
                diagonal = lax.broadcasted_iota(jnp.int32, dots.shape, 0) == lax.broadcasted_iota(
                    jnp.int32, dots.shape, 1
                )
                same = jnp.logical_and(diagonal, hh == a)
                sign = jnp.where(same, 1.0, -1.0)
                grad = -sign * jax.nn.sigmoid(-sign * logits) / PAIRS
            else:
                grad = jax.nn.sigmoid(logits) / PAIRS
            offset = 2 * j + hh - a
            met = jnp.logical_and(offset >= 0, offset < STEPS)
            weights[a, :, cols] = jnp.where(met, scale * grad, 0.0).astype(BF16)

    for k, a in ((0, 1 - hh), (1, hh)):
        weighted = weights[a]

        def column(i, c, k=k, weighted=weighted):
            cols = pl.ds(pl.multiple_of(i * 256, 256), 256)
            acc[k, :, cols] = jnp.dot(weighted, buf[:, cols], preferred_element_type=F32)
            return c

        lax.fori_loop(0, E // 256, column, 0)
        if k == 0:
            send(acc.at[0], d_recv, d_ss, d_rs, sibling)
    arrived(d_recv, d_rs)
    d_own = acc[1] + d_recv[...]
    unit = y_own[...]
    up = (inv_own[...] * (d_own - unit * jnp.sum(unit * d_own, axis=-1, keepdims=True))).astype(BF16)
    dy[...] = up
    for k in range(NY):
        dy_slices[k] = up[:, k * SLICE : (k + 1) * SLICE]
    send(dy, dy_other, x2_ss, x2_rs, partner)
    for d in range(1, NY):
        to = (y + d) % NY
        send(dy_slices.at[to], dyg.at[mine], dg_ss.at[d - 1], dg_rs.at[mine], at(xl, z, to, h, r))
    dyg[mine] = dy_slices[y]
    send(dyg.at[mine], dyg.at[mine], dg_ss.at[3], dg_rs.at[mine], sibling)

    def input_grad(dy_ref, tower):
        def column(i, c):
            cols = pl.ds(pl.multiple_of(i * 256, 256), 256)
            gx[tower, :, cols] = contract(dy_ref[...], w[tower, cols, :], 1, 1).astype(BF16)
            return c

        lax.fori_loop(0, HALF // 256, column, 0)

    input_grad(dy, r)
    for d in range(1, NY):
        slot = 2 * ((y + d) % NY) + h
        arrived(dyg.at[slot], dg_rs.at[slot])
        send(dyg.at[slot], dyg.at[slot], dg_ss.at[3 + d], dg_rs.at[slot], sibling)
    for d in range(NY):
        slot = 2 * ((y + d) % NY) + 1 - h
        arrived(dyg.at[slot], dg_rs.at[slot])

    for slot in range(8):
        @pl.when(jnp.logical_or(hh == 0, slot // 2 != y))
        def _():
            arrived(xg.at[slot], xg_rs.at[slot])

    ups = dyg[...].reshape(8 * ROWS, SLICE)

    def weight_rows(i, c):
        cols = pl.ds(pl.multiple_of(i * 384, 128), 384)
        g = contract(xg[:, :, cols].reshape(8 * ROWS, 384), ups, 0, 0)
        g_send[i] = g.astype(BF16)
        return c

    lax.fori_loop(0, 2, weight_rows, 0)
    send(g_send.at[1 - xl], xr.at[xl], xr_ss.at[0], xr_rs.at[xl], across)
    send(g_send.at[xl], xr.at[xl], xr_ss.at[1], xr_rs.at[xl], at(xl, z, y, r, h), hh == 1)

    @pl.when(hh == 0)
    def _():
        pltpu.make_async_copy(g_send.at[xl], xr.at[xl], xr_rs.at[xl]).start()

    arrived(dy_other, x2_rs)
    input_grad(dy_other, 1 - r)
    gxi_ref[...] = gx[0]
    gxt_ref[...] = gx[1]

    for k in range(2):
        arrived(xr.at[k], xr_rs.at[k])
    z_send[...] = (xr[0].astype(F32) + xr[1].astype(F32)).astype(BF16).reshape(NZ, 48, SLICE)
    for d in range(1, NZ):
        to = (z + d) % NZ
        send(z_send.at[to], zr.at[z], z_ss.at[d - 1], z_rs.at[z], at(xl, to, y, h, r))
    total = z_send[z].astype(F32)
    for d in range(1, NZ):
        slot = (z + d) % NZ
        arrived(zr.at[slot], z_rs.at[slot])
        total = total + zr[slot].astype(F32)
    for k in range(8):
        f_send[k, 0:6, :] = total[6 * k : 6 * k + 6, :]
        f_send[k, 6:8, :] = jnp.zeros((2, SLICE), F32)
    f_recv[h, y] = f_send[mine]
    for d in range(NY):
        to = (y + d) % NY
        for c in range(2):
            if d == 0 and c == 0:
                continue
            core = (h + c) % 2
            send(
                f_send.at[2 * to + core], f_recv.at[h, y], f_ss.at[2 * d + c], f_rs.at[h, y],
                at(xl, z, to, core, r),
            )
    for d in range(NY):
        for c in range(2):
            if d == 0 and c == 0:
                continue
            core, frm = (h + c) % 2, (y + d) % NY
            arrived(f_recv.at[core, frm], f_rs.at[core, frm])
    for k in range(NY):
        cols = pl.ds(k * SLICE, SLICE)
        gwi_ref[:, cols] = f_recv[0, k, 0:6, :]
        gwt_ref[:, cols] = f_recv[1, k, 0:6, :]
    for finish in pending:
        finish()


def local(image_in, text_in, image_w, text_w, logit_scale, logit_bias):
    hbm = pl.BlockSpec(memory_space=pl.ANY)
    vmem = pl.BlockSpec(memory_space=pltpu.VMEM)
    smem = pl.BlockSpec(memory_space=pltpu.SMEM)
    dma = pltpu.SemaphoreType.DMA
    return pl.pallas_call(
        body,
        name="contrast",
        out_shape=(
            jax.ShapeDtypeStruct((ROWS, HALF), BF16),
            jax.ShapeDtypeStruct((ROWS, HALF), BF16),
            jax.ShapeDtypeStruct((6, E), F32),
            jax.ShapeDtypeStruct((6, E), F32),
        ),
        in_specs=[hbm] * 4 + [smem] * 2,
        out_specs=(vmem,) * 4,
        scratch_shapes=[
            pltpu.VMEM((2, ROWS, HALF), BF16),
            pltpu.VMEM((2, HALF, E), BF16),
            pltpu.VMEM((2, ROWS, E), F32),
            pltpu.VMEM((2, ROWS, E), BF16),
            pltpu.VMEM((2, ROWS, E), BF16),
            pltpu.VMEM((SLOTS * ROWS, E), BF16),
            pltpu.VMEM((2, ROWS, E), BF16),
            pltpu.VMEM((ROWS, E), F32),
            pltpu.VMEM((ROWS, 1), F32),
            pltpu.VMEM((2, ROWS, SLOTS * ROWS), BF16),
            pltpu.VMEM((2, ROWS, E), F32),
            pltpu.VMEM((ROWS, E), F32),
            pltpu.VMEM((ROWS, E), BF16),
            pltpu.VMEM((NY, ROWS, SLICE), BF16),
            pltpu.VMEM((ROWS, E), BF16),
            pltpu.VMEM((2, ROWS, HALF), BF16),
            pltpu.VMEM((8, ROWS, HALF), BF16),
            pltpu.VMEM((8, ROWS, SLICE), BF16),
            pltpu.VMEM((2, HALF // 2, SLICE), BF16),
            pltpu.VMEM((2, HALF // 2, SLICE), BF16),
            pltpu.VMEM((NZ, 48, SLICE), BF16),
            pltpu.VMEM((NZ, 48, SLICE), BF16),
            pltpu.VMEM((8, 8, SLICE), F32),
            pltpu.VMEM((2, NY, 8, SLICE), F32),
            dma((4,)),
            dma((11,)),
            dma((8,)),
            dma((2, NCH)),
            dma((2, NCH)),
            dma((2, NCH)),
            dma((3, 3, NCH)),
            dma((SLOTS, NCH)),
            dma, dma,
            dma, dma,
            dma, dma,
            dma((7,)),
            dma((8,)),
            dma((2,)),
            dma((2,)),
            dma((7,)),
            dma((8,)),
            dma((8,)),
            dma((2, NY)),
        ],
        compiler_params=pltpu.CompilerParams(
            collective_id=0, has_side_effects=True, vmem_limit_bytes=48 << 20
        ),
    )(image_in, text_in, image_w, text_w, logit_scale.reshape(1, 1), logit_bias.reshape(1, 1))


def solution(mesh):
    placed = (P("dp", "mp"), P("dp", "mp"), P("mp", None), P("mp", None), P(), P())
    return jax.shard_map(
        local,
        mesh=mesh,
        in_specs=placed,
        out_specs=(P("dp", "mp"), P("dp", "mp"), P(("mp", "dp"), None), P(("mp", "dp"), None)),
        check_vma=False,
    )
```

```python
import jax
import jax.numpy as jnp
from jax import lax
from jax.experimental import pallas as pl
from jax.experimental.pallas import tpu as pltpu
from jax.sharding import PartitionSpec as P

MESH = pl.DeviceIdType.MESH
F32, BF16 = jnp.float32, jnp.bfloat16
ROWS = 128
HALF = 768
E = 1536
NY, NZ = 4, 8
SLICE = E // NY
STEPS = 16
SLOTS = 9
NCH = 8
CH = ROWS // NCH
PAIRS = 16384.0


def contract(a, b, da, db):
    return lax.dot_general(a, b, (((da,), (db,)), ((), ())), preferred_element_type=F32)


def body(
    image_in, text_in, image_w, text_w, scale_ref, bias_ref,
    gxi_ref, gxt_ref, gwi_ref, gwt_ref,
    x, w, part, px_send, px_recv, buf, own, y_own, inv_own, weights, acc, d_recv,
    dy, dy_slices, dy_other, gx, xg, dyg, g_send, xr, z_send, zr, f_send, f_recv,
    ld_sem, xg_ss, xg_rs, px_ss, px_rs, zs_ss, ys_ss, bf_rs, ow_ss, ow_rs, d_ss, d_rs,
    x2_ss, x2_rs, dg_ss, dg_rs, xr_ss, xr_rs, z_ss, z_rs, f_ss, f_rs,
):
    dp, r = lax.axis_index("dp"), lax.axis_index("mp")
    h, y, z, xl = dp % 2, (dp // 2) % NY, (dp // 8) % NZ, dp // 64
    m = dp + r * (127 - 2 * dp)
    hh, my, plane = m % 2, (m // 2) % NY, m // 8

    def at(xl_, z_, y_, core, mp):
        return (((xl_ * NZ + z_) * NY + y_) * 2 + core, mp)

    def mirrored(m_):
        return (m_ + r * (127 - 2 * m_), r)

    sibling = at(xl, z, y, 1 - h, r)
    partner = at(xl, z, y, h, 1 - r)
    across = at(1 - xl, z, y, r, h)

    pending = []

    def send(src, dst, ss, rs, device, when=None):
        def copy():
            return pltpu.make_async_remote_copy(
                src_ref=src, dst_ref=dst, send_sem=ss, recv_sem=rs, device_id=device, device_id_type=MESH
            )

        if when is None:
            copy().start()
            pending.append(lambda: copy().wait_send())
        else:

            @pl.when(when)
            def _():
                copy().start()

            def finish():
                @pl.when(when)
                def _():
                    copy().wait_send()

            pending.append(finish)

    def arrived(dst, rs):
        pltpu.make_async_copy(dst, dst, rs).wait()

    def load(src, dst, i):
        copy = pltpu.make_async_copy(src, dst, ld_sem.at[i])
        copy.start()
        return copy

    loads = [
        load(image_in, x.at[0], 0),
        load(text_in, x.at[1], 1),
        load(image_w, w.at[0], 2),
        load(text_w, w.at[1], 3),
    ]
    bar = pltpu.get_barrier_semaphore()
    peers = [sibling, partner, at(xl, z, y, 1 - h, 1 - r), across]
    peers += [at(xl, z, (y + d) % NY, c, r) for d in range(1, NY) for c in (0, 1)]
    peers += [at(xl, (z + d) % NZ, y, h, r) for d in range(1, NZ)]
    peers += [mirrored((m + 8) % 128), mirrored((m + 120) % 128)]
    for peer in peers:
        pl.semaphore_signal(bar, inc=1, device_id=peer, device_id_type=MESH)
    for copy in loads[:2]:
        copy.wait()
    pl.semaphore_wait(bar, len(peers))

    mine = 2 * y + h
    for d in range(1, NY):
        send(x.at[r], xg.at[mine], xg_ss.at[d], xg_rs.at[mine], at(xl, z, (y + d) % NY, r, r))
    send(x.at[r], xg.at[mine], xg_ss.at[4], xg_rs.at[mine], sibling, hh == 1)

    @pl.when(hh == 0)
    def _():
        pltpu.make_async_copy(x.at[r], xg.at[mine], xg_rs.at[mine]).start()

    for copy in loads[2:]:
        copy.wait()

    def project(k, tower):
        features = x[tower]

        def column(i, c):
            cols = pl.ds(pl.multiple_of(i * 256, 256), 256)
            p = jnp.dot(features, w[tower, :, cols], preferred_element_type=F32)
            part[k, :, cols] = p
            px_send[k, :, cols] = p.astype(BF16)
            return c

        lax.fori_loop(0, E // 256, column, 0)

    def send_part(k, c):
        rows = pl.ds(c * CH, CH)
        send(px_send.at[k, rows], px_recv.at[k, rows], px_ss.at[k, c], px_rs.at[k, c], partner)

    project(0, r)
    PX0 = len(pending)
    for c in range(3):
        send_part(0, c)
    project(1, 1 - r)
    for c in range(3, NCH):
        pending.pop(PX0)()
        send_part(0, c)

    def slot_rows(j, c):
        return pl.ds(pl.multiple_of(j * ROWS + c * CH, CH), CH)

    def y_peer(d):
        return mirrored(plane * 8 + ((my + d) % NY) * 2 + hh)

    z_peer = mirrored((m + 120) % 128)

    def pass_z(j, k, c, when=None):
        src = buf.at[slot_rows(j, c)]
        send(src, buf.at[slot_rows(j + 4, c)], zs_ss.at[k, c], bf_rs.at[j + 4, c], z_peer, when)

    def pass_y(j, d, k, c, slot, when=None):
        src = buf.at[slot_rows(j, c)]
        send(src, buf.at[slot_rows(slot, c)], ys_ss.at[k, d - 1, c], bf_rs.at[slot, c], y_peer(d), when)

    def block(j, c):
        arrived(buf.at[slot_rows(j, c)], bf_rs.at[j, c])

    last_plane = plane % NZ == NZ - 1

    for c in range(NCH):
        rows = pl.ds(c * CH, CH)
        arrived(px_recv.at[0, rows], px_rs.at[0, c])
        if c == NCH - 1:
            for k in range(NCH):
                send_part(1, k)
        yy = part[1, rows, :] + px_recv[0, rows, :].astype(F32)
        inv = lax.rsqrt(jnp.sum(yy * yy, axis=-1, keepdims=True) + 1e-06)
        buf[slot_rows(0, c), :] = (yy * inv).astype(BF16)
        pass_z(0, 0, c)
        for d in (2, 1, 3):
            pass_y(0, d, 0, c, 4 - d, my + d >= NY)
    for c in range(NCH):
        block(4, c)
        pass_z(4, 1, c)
        pass_y(4, 2, 1, c, 2 + 4 * ((my + 2) // NY), jnp.logical_or(my + 2 < NY, last_plane))
        for d in (1, 3):
            pass_y(4, d, 1, c, 4 - d + 4 * ((my + d) // NY))
    for c in range(NCH):
        block(2, c)
        pass_z(2, 2, c, plane % NZ != 0)
    for c in range(NCH):
        block(8, c)
        for d in (1, 3):
            pass_y(8, d, 2, c, 8 - d, my + d < NY)
        pass_y(8, 2, 2, c, 6, jnp.logical_and(my + 2 < NY, last_plane))
    send(x.at[1 - r], xg.at[mine], xg_ss.at[0], xg_rs.at[mine], at(xl, z, y, r, 1 - r))
    for c in range(NCH):
        rows = pl.ds(c * CH, CH)
        arrived(px_recv.at[1, rows], px_rs.at[1, c])
        yy = part[0, rows, :] + px_recv[1, rows, :].astype(F32)
        inv = lax.rsqrt(jnp.sum(yy * yy, axis=-1, keepdims=True) + 1e-06)
        unit = yy * inv
        y_own[rows, :] = unit
        inv_own[rows, :] = inv
        own[hh, rows, :] = unit.astype(BF16)
    send(own.at[hh], own.at[hh], ow_ss, ow_rs, sibling)
    arrived(own.at[1 - hh], ow_rs)

    scale, bias = scale_ref[0, 0], bias_ref[0, 0]
    for j in (0, 4, 8, 2, 3, 1, 7, 5, 6):
        if j not in (0, 4, 8, 2):
            for c in range(NCH):
                block(j, c)
        cols = pl.ds(j * ROWS, ROWS)
        for a in range(2):
            dots = contract(own[a], buf[cols, :], 1, 1)
            logits = scale * dots + bias
            if j == 0:
                diagonal = lax.broadcasted_iota(jnp.int32, dots.shape, 0) == lax.broadcasted_iota(
                    jnp.int32, dots.shape, 1
                )
                same = jnp.logical_and(diagonal, hh == a)
                sign = jnp.where(same, 1.0, -1.0)
                grad = -sign * jax.nn.sigmoid(-sign * logits) / PAIRS
            else:
                grad = jax.nn.sigmoid(logits) / PAIRS
            offset = 2 * j + hh - a
            met = jnp.logical_and(offset >= 0, offset < STEPS)
            weights[a, :, cols] = jnp.where(met, scale * grad, 0.0).astype(BF16)

    for c in range(2):
        slot = 2 * y + c

        @pl.when(hh == 1)
        def _():
            arrived(xg.at[slot], xg_rs.at[slot])

        for d in range(1, NY):
            send(
                xg.at[slot], xg.at[slot], xg_ss.at[4 + 3 * c + d], xg_rs.at[slot],
                at(xl, z, (y + d) % NY, h, r), hh == 1,
            )

    for k, a in ((0, 1 - hh), (1, hh)):
        weighted = weights[a]

        def column(i, c, k=k, weighted=weighted):
            cols = pl.ds(pl.multiple_of(i * 256, 256), 256)
            acc[k, :, cols] = jnp.dot(weighted, buf[:, cols], preferred_element_type=F32)
            return c

        lax.fori_loop(0, E // 256, column, 0)
        if k == 0:
            send(acc.at[0], d_recv, d_ss, d_rs, sibling)
    arrived(d_recv, d_rs)
    d_own = acc[1] + d_recv[...]
    unit = y_own[...]
    up = (inv_own[...] * (d_own - unit * jnp.sum(unit * d_own, axis=-1, keepdims=True))).astype(BF16)
    dy[...] = up
    for k in range(NY):
        dy_slices[k] = up[:, k * SLICE : (k + 1) * SLICE]
    send(dy, dy_other, x2_ss, x2_rs, partner)
    for d in range(1, NY):
        to = (y + d) % NY
        send(dy_slices.at[to], dyg.at[mine], dg_ss.at[d - 1], dg_rs.at[mine], at(xl, z, to, h, r))
    dyg[mine] = dy_slices[y]
    send(dyg.at[mine], dyg.at[mine], dg_ss.at[3], dg_rs.at[mine], sibling)

    def input_grad(dy_ref, tower):
        def column(i, c):
            cols = pl.ds(pl.multiple_of(i * 256, 256), 256)
            gx[tower, :, cols] = contract(dy_ref[...], w[tower, cols, :], 1, 1).astype(BF16)
            return c

        lax.fori_loop(0, HALF // 256, column, 0)

    input_grad(dy, r)
    for d in range(1, NY):
        slot = 2 * ((y + d) % NY) + h
        arrived(dyg.at[slot], dg_rs.at[slot])
        send(dyg.at[slot], dyg.at[slot], dg_ss.at[3 + d], dg_rs.at[slot], sibling)
    for d in range(NY):
        slot = 2 * ((y + d) % NY) + 1 - h
        arrived(dyg.at[slot], dg_rs.at[slot])

    for slot in range(8):
        @pl.when(jnp.logical_or(hh == 0, slot // 2 != y))
        def _():
            arrived(xg.at[slot], xg_rs.at[slot])

    ups = dyg[...].reshape(8 * ROWS, SLICE)

    def weight_rows(i, c):
        cols = pl.ds(pl.multiple_of(i * 384, 128), 384)
        g = contract(xg[:, :, cols].reshape(8 * ROWS, 384), ups, 0, 0)
        g_send[i] = g.astype(BF16)
        return c

    lax.fori_loop(0, 2, weight_rows, 0)
    send(g_send.at[1 - xl], xr.at[xl], xr_ss.at[0], xr_rs.at[xl], across)
    send(g_send.at[xl], xr.at[xl], xr_ss.at[1], xr_rs.at[xl], at(xl, z, y, r, h), hh == 1)

    @pl.when(hh == 0)
    def _():
        pltpu.make_async_copy(g_send.at[xl], xr.at[xl], xr_rs.at[xl]).start()

    arrived(dy_other, x2_rs)
    input_grad(dy_other, 1 - r)
    gxi_ref[...] = gx[0]
    gxt_ref[...] = gx[1]

    for k in range(2):
        arrived(xr.at[k], xr_rs.at[k])
    z_send[...] = (xr[0].astype(F32) + xr[1].astype(F32)).astype(BF16).reshape(NZ, 48, SLICE)
    for d in range(1, NZ):
        to = (z + d) % NZ
        send(z_send.at[to], zr.at[z], z_ss.at[d - 1], z_rs.at[z], at(xl, to, y, h, r))
    total = z_send[z].astype(F32)
    for d in range(1, NZ):
        slot = (z + d) % NZ
        arrived(zr.at[slot], z_rs.at[slot])
        total = total + zr[slot].astype(F32)
    for k in range(8):
        f_send[k, 0:6, :] = total[6 * k : 6 * k + 6, :]
        f_send[k, 6:8, :] = jnp.zeros((2, SLICE), F32)
    f_recv[h, y] = f_send[mine]
    for d in range(NY):
        to = (y + d) % NY
        for c in range(2):
            if d == 0 and c == 0:
                continue
            core = (h + c) % 2
            send(
                f_send.at[2 * to + core], f_recv.at[h, y], f_ss.at[2 * d + c], f_rs.at[h, y],
                at(xl, z, to, core, r),
            )
    for d in range(NY):
        for c in range(2):
            if d == 0 and c == 0:
                continue
            core, frm = (h + c) % 2, (y + d) % NY
            arrived(f_recv.at[core, frm], f_rs.at[core, frm])
    for k in range(NY):
        cols = pl.ds(k * SLICE, SLICE)
        gwi_ref[:, cols] = f_recv[0, k, 0:6, :]
        gwt_ref[:, cols] = f_recv[1, k, 0:6, :]
    for finish in pending:
        finish()


def hand_over(*refs):
    for i in range(4):
        refs[4 + i][...] = refs[i][...]


def local(image_in, text_in, image_w, text_w, logit_scale, logit_bias):
    hbm = pl.BlockSpec(memory_space=pltpu.HBM)
    vmem = pl.BlockSpec(memory_space=pltpu.VMEM)
    smem = pl.BlockSpec(memory_space=pltpu.SMEM)
    dma = pltpu.SemaphoreType.DMA
    results = pl.pallas_call(
        body,
        name="contrast",
        out_shape=(
            jax.ShapeDtypeStruct((ROWS, HALF), BF16),
            jax.ShapeDtypeStruct((ROWS, HALF), BF16),
            jax.ShapeDtypeStruct((6, E), F32),
            jax.ShapeDtypeStruct((6, E), F32),
        ),
        in_specs=[hbm] * 4 + [smem] * 2,
        out_specs=(vmem,) * 4,
        scratch_shapes=[
            pltpu.VMEM((2, ROWS, HALF), BF16),
            pltpu.VMEM((2, HALF, E), BF16),
            pltpu.VMEM((2, ROWS, E), F32),
            pltpu.VMEM((2, ROWS, E), BF16),
            pltpu.VMEM((2, ROWS, E), BF16),
            pltpu.VMEM((SLOTS * ROWS, E), BF16),
            pltpu.VMEM((2, ROWS, E), BF16),
            pltpu.VMEM((ROWS, E), F32),
            pltpu.VMEM((ROWS, 1), F32),
            pltpu.VMEM((2, ROWS, SLOTS * ROWS), BF16),
            pltpu.VMEM((2, ROWS, E), F32),
            pltpu.VMEM((ROWS, E), F32),
            pltpu.VMEM((ROWS, E), BF16),
            pltpu.VMEM((NY, ROWS, SLICE), BF16),
            pltpu.VMEM((ROWS, E), BF16),
            pltpu.VMEM((2, ROWS, HALF), BF16),
            pltpu.VMEM((8, ROWS, HALF), BF16),
            pltpu.VMEM((8, ROWS, SLICE), BF16),
            pltpu.VMEM((2, HALF // 2, SLICE), BF16),
            pltpu.VMEM((2, HALF // 2, SLICE), BF16),
            pltpu.VMEM((NZ, 48, SLICE), BF16),
            pltpu.VMEM((NZ, 48, SLICE), BF16),
            pltpu.VMEM((8, 8, SLICE), F32),
            pltpu.VMEM((2, NY, 8, SLICE), F32),
            dma((4,)),
            dma((11,)),
            dma((8,)),
            dma((2, NCH)),
            dma((2, NCH)),
            dma((3, NCH)),
            dma((3, 3, NCH)),
            dma((SLOTS, NCH)),
            dma, dma,
            dma, dma,
            dma, dma,
            dma((7,)),
            dma((8,)),
            dma((2,)),
            dma((2,)),
            dma((7,)),
            dma((8,)),
            dma((8,)),
            dma((2, NY)),
        ],
        compiler_params=pltpu.CompilerParams(
            collective_id=0, has_side_effects=True, vmem_limit_bytes=60 << 20
        ),
    )(image_in, text_in, image_w, text_w, logit_scale.reshape(1, 1), logit_bias.reshape(1, 1))
    return pl.pallas_call(
        hand_over,
        name="hand_over",
        out_shape=tuple(jax.ShapeDtypeStruct(q.shape, q.dtype) for q in results),
        in_specs=[vmem] * 4,
        out_specs=(vmem,) * 4,
    )(*results)


def solution(mesh):
    placed = (P("dp", "mp"), P("dp", "mp"), P("mp", None), P("mp", None), P(), P())
    return jax.shard_map(
        local,
        mesh=mesh,
        in_specs=placed,
        out_specs=(P("dp", "mp"), P("dp", "mp"), P(("mp", "dp"), None), P(("mp", "dp"), None)),
        check_vma=False,
    )
```

```python
import jax
import jax.numpy as jnp
from jax import lax
from jax.experimental import pallas as pl
from jax.experimental.pallas import tpu as pltpu
from jax.sharding import PartitionSpec as P

MESH = pl.DeviceIdType.MESH
F32, BF16 = jnp.float32, jnp.bfloat16
ROWS = 128
HALF = 768
E = 1536
NY, NZ = 4, 8
SLICE = E // NY
STEPS = 16
SLOTS = 9
NCH = 8
CH = ROWS // NCH
PAIRS = 16384.0


def contract(a, b, da, db):
    return lax.dot_general(a, b, (((da,), (db,)), ((), ())), preferred_element_type=F32)


def body(
    image_in, text_in, image_w, text_w, scale_ref, bias_ref,
    gxi_ref, gxt_ref, gwi_ref, gwt_ref,
    x, w, part, px_send, px_recv, buf, own, y_own, inv_own, weights, acc, d_recv,
    dy, dy_slices, dy_other, gx, xg, dyg, g_send, xr, z_send, zr, f_send, f_recv,
    ld_sem, xg_ss, xg_rs, px_ss, px_rs, zs_ss, ys_ss, bf_rs, ow_ss, ow_rs, d_ss, d_rs,
    x2_ss, x2_rs, dg_ss, dg_rs, xr_ss, xr_rs, z_ss, z_rs, f_ss, f_rs,
):
    dp, r = lax.axis_index("dp"), lax.axis_index("mp")
    h, y, z, xl = dp % 2, (dp // 2) % NY, (dp // 8) % NZ, dp // 64
    m = dp + r * (127 - 2 * dp)
    hh, my, plane = m % 2, (m // 2) % NY, m // 8

    def at(xl_, z_, y_, core, mp):
        return (((xl_ * NZ + z_) * NY + y_) * 2 + core, mp)

    def mirrored(m_):
        return (m_ + r * (127 - 2 * m_), r)

    sibling = at(xl, z, y, 1 - h, r)
    partner = at(xl, z, y, h, 1 - r)
    across = at(1 - xl, z, y, r, h)

    pending = []

    def send(src, dst, ss, rs, device, when=None):
        def copy():
            return pltpu.make_async_remote_copy(
                src_ref=src, dst_ref=dst, send_sem=ss, recv_sem=rs, device_id=device, device_id_type=MESH
            )

        if when is None:
            copy().start()
            pending.append(lambda: copy().wait_send())
        else:

            @pl.when(when)
            def _():
                copy().start()

            def finish():
                @pl.when(when)
                def _():
                    copy().wait_send()

            pending.append(finish)

    def arrived(dst, rs):
        pltpu.make_async_copy(dst, dst, rs).wait()

    def load(src, dst, i):
        copy = pltpu.make_async_copy(src, dst, ld_sem.at[i])
        copy.start()
        return copy

    loads = [
        load(image_in, x.at[0], 0),
        load(text_in, x.at[1], 1),
        load(image_w, w.at[0], 2),
        load(text_w, w.at[1], 3),
    ]
    bar = pltpu.get_barrier_semaphore()
    peers = [sibling, partner, at(xl, z, y, 1 - h, 1 - r), across]
    peers += [at(xl, z, (y + d) % NY, c, r) for d in range(1, NY) for c in (0, 1)]
    peers += [at(xl, (z + d) % NZ, y, h, r) for d in range(1, NZ)]
    peers += [mirrored((m + 8) % 128), mirrored((m + 120) % 128)]
    for peer in peers:
        pl.semaphore_signal(bar, inc=1, device_id=peer, device_id_type=MESH)
    for copy in loads[:2]:
        copy.wait()
    pl.semaphore_wait(bar, len(peers))

    mine = 2 * y + h
    for d in range(1, NY):
        send(x.at[r], xg.at[mine], xg_ss.at[d], xg_rs.at[mine], at(xl, z, (y + d) % NY, r, r))
    send(x.at[r], xg.at[mine], xg_ss.at[4], xg_rs.at[mine], sibling, hh == 1)

    @pl.when(hh == 0)
    def _():
        pltpu.make_async_copy(x.at[r], xg.at[mine], xg_rs.at[mine]).start()

    for copy in loads[2:]:
        copy.wait()

    def project(k, tower):
        features = x[tower]

        def column(i, c):
            cols = pl.ds(pl.multiple_of(i * 256, 256), 256)
            p = jnp.dot(features, w[tower, :, cols], preferred_element_type=F32)
            part[k, :, cols] = p
            px_send[k, :, cols] = p.astype(BF16)
            return c

        lax.fori_loop(0, E // 256, column, 0)

    def send_part(k, c):
        rows = pl.ds(c * CH, CH)
        send(px_send.at[k, rows], px_recv.at[k, rows], px_ss.at[k, c], px_rs.at[k, c], partner)

    project(0, r)
    PX0 = len(pending)
    for c in range(3):
        send_part(0, c)
    project(1, 1 - r)
    for c in range(3, NCH):
        pending.pop(PX0)()
        send_part(0, c)

    def slot_rows(j, c):
        return pl.ds(pl.multiple_of(j * ROWS + c * CH, CH), CH)

    def y_peer(d):
        return mirrored(plane * 8 + ((my + d) % NY) * 2 + hh)

    z_peer = mirrored((m + 120) % 128)

    def pass_z(j, k, c, when=None):
        src = buf.at[slot_rows(j, c)]
        send(src, buf.at[slot_rows(j + 4, c)], zs_ss.at[k, c], bf_rs.at[j + 4, c], z_peer, when)

    def pass_y(j, d, k, c, slot, when=None):
        src = buf.at[slot_rows(j, c)]
        send(src, buf.at[slot_rows(slot, c)], ys_ss.at[k, d - 1, c], bf_rs.at[slot, c], y_peer(d), when)

    def block(j, c):
        arrived(buf.at[slot_rows(j, c)], bf_rs.at[j, c])

    last_plane = plane % NZ == NZ - 1

    for c in range(NCH):
        rows = pl.ds(c * CH, CH)
        arrived(px_recv.at[0, rows], px_rs.at[0, c])
        if c == NCH - 1:
            for k in range(NCH):
                send_part(1, k)
        yy = part[1, rows, :] + px_recv[0, rows, :].astype(F32)
        inv = lax.rsqrt(jnp.sum(yy * yy, axis=-1, keepdims=True) + 1e-06)
        buf[slot_rows(0, c), :] = (yy * inv).astype(BF16)
        pass_z(0, 0, c)
        for d in (2, 1, 3):
            pass_y(0, d, 0, c, 4 - d, my + d >= NY)
    for c in range(NCH):
        block(4, c)
        pass_z(4, 1, c)
        pass_y(4, 2, 1, c, 2 + 4 * ((my + 2) // NY), jnp.logical_or(my + 2 < NY, last_plane) if c % 2 == 1 else my + 2 < NY)
        for d in (1, 3):
            pass_y(4, d, 1, c, 4 - d + 4 * ((my + d) // NY))
    for c in range(NCH):
        block(2, c)
        pass_z(2, 2, c, (plane % NZ != 0) if c % 2 == 1 else None)
    for c in range(NCH):
        block(8, c)
        for d in (1, 3):
            pass_y(8, d, 2, c, 8 - d, my + d < NY)
        if c % 2 == 1:
            pass_y(8, 2, 2, c, 6, jnp.logical_and(my + 2 < NY, last_plane))
    send(x.at[1 - r], xg.at[mine], xg_ss.at[0], xg_rs.at[mine], at(xl, z, y, r, 1 - r))
    for c in range(NCH):
        rows = pl.ds(c * CH, CH)
        arrived(px_recv.at[1, rows], px_rs.at[1, c])
        yy = part[0, rows, :] + px_recv[1, rows, :].astype(F32)
        inv = lax.rsqrt(jnp.sum(yy * yy, axis=-1, keepdims=True) + 1e-06)
        unit = yy * inv
        y_own[rows, :] = unit
        inv_own[rows, :] = inv
        own[hh, rows, :] = unit.astype(BF16)
    send(own.at[hh], own.at[hh], ow_ss, ow_rs, sibling)
    arrived(own.at[1 - hh], ow_rs)

    scale, bias = scale_ref[0, 0], bias_ref[0, 0]
    for j in (0, 4, 8, 2, 3, 1, 7, 5, 6):
        if j not in (0, 4, 8, 2):
            for c in range(NCH):
                block(j, c)
        cols = pl.ds(j * ROWS, ROWS)
        for a in range(2):
            dots = contract(own[a], buf[cols, :], 1, 1)
            logits = scale * dots + bias
            if j == 0:
                diagonal = lax.broadcasted_iota(jnp.int32, dots.shape, 0) == lax.broadcasted_iota(
                    jnp.int32, dots.shape, 1
                )
                same = jnp.logical_and(diagonal, hh == a)
                sign = jnp.where(same, 1.0, -1.0)
                grad = -sign * jax.nn.sigmoid(-sign * logits) / PAIRS
            else:
                grad = jax.nn.sigmoid(logits) / PAIRS
            offset = 2 * j + hh - a
            met = jnp.logical_and(offset >= 0, offset < STEPS)
            weights[a, :, cols] = jnp.where(met, scale * grad, 0.0).astype(BF16)

    for c in range(2):
        slot = 2 * y + c

        @pl.when(hh == 1)
        def _():
            arrived(xg.at[slot], xg_rs.at[slot])

        for d in range(1, NY):
            send(
                xg.at[slot], xg.at[slot], xg_ss.at[4 + 3 * c + d], xg_rs.at[slot],
                at(xl, z, (y + d) % NY, h, r), hh == 1,
            )

    for k, a in ((0, 1 - hh), (1, hh)):
        weighted = weights[a]

        def column(i, c, k=k, weighted=weighted):
            cols = pl.ds(pl.multiple_of(i * 256, 256), 256)
            acc[k, :, cols] = jnp.dot(weighted, buf[:, cols], preferred_element_type=F32)
            return c

        lax.fori_loop(0, E // 256, column, 0)
        if k == 0:
            send(acc.at[0], d_recv, d_ss, d_rs, sibling)
    arrived(d_recv, d_rs)
    d_own = acc[1] + d_recv[...]
    unit = y_own[...]
    up = (inv_own[...] * (d_own - unit * jnp.sum(unit * d_own, axis=-1, keepdims=True))).astype(BF16)
    dy[...] = up
    for k in range(NY):
        dy_slices[k] = up[:, k * SLICE : (k + 1) * SLICE]
    send(dy, dy_other, x2_ss, x2_rs, partner)
    for d in range(1, NY):
        to = (y + d) % NY
        send(dy_slices.at[to], dyg.at[mine], dg_ss.at[d - 1], dg_rs.at[mine], at(xl, z, to, h, r))
    dyg[mine] = dy_slices[y]
    send(dyg.at[mine], dyg.at[mine], dg_ss.at[3], dg_rs.at[mine], sibling)

    def input_grad(dy_ref, tower):
        def column(i, c):
            cols = pl.ds(pl.multiple_of(i * 256, 256), 256)
            gx[tower, :, cols] = contract(dy_ref[...], w[tower, cols, :], 1, 1).astype(BF16)
            return c

        lax.fori_loop(0, HALF // 256, column, 0)

    input_grad(dy, r)
    for d in range(1, NY):
        slot = 2 * ((y + d) % NY) + h
        arrived(dyg.at[slot], dg_rs.at[slot])
        send(dyg.at[slot], dyg.at[slot], dg_ss.at[3 + d], dg_rs.at[slot], sibling)
    for d in range(NY):
        slot = 2 * ((y + d) % NY) + 1 - h
        arrived(dyg.at[slot], dg_rs.at[slot])

    for slot in range(8):
        @pl.when(jnp.logical_or(hh == 0, slot // 2 != y))
        def _():
            arrived(xg.at[slot], xg_rs.at[slot])

    ups = dyg[...].reshape(8 * ROWS, SLICE)

    def weight_rows(i, c):
        cols = pl.ds(pl.multiple_of(i * 384, 128), 384)
        g = contract(xg[:, :, cols].reshape(8 * ROWS, 384), ups, 0, 0)
        g_send[i] = g.astype(BF16)
        return c

    lax.fori_loop(0, 2, weight_rows, 0)
    send(g_send.at[1 - xl], xr.at[xl], xr_ss.at[0], xr_rs.at[xl], across)
    send(g_send.at[xl], xr.at[xl], xr_ss.at[1], xr_rs.at[xl], at(xl, z, y, r, h), hh == 1)

    @pl.when(hh == 0)
    def _():
        pltpu.make_async_copy(g_send.at[xl], xr.at[xl], xr_rs.at[xl]).start()

    arrived(dy_other, x2_rs)
    input_grad(dy_other, 1 - r)
    gxi_ref[...] = gx[0]
    gxt_ref[...] = gx[1]

    for k in range(2):
        arrived(xr.at[k], xr_rs.at[k])
    z_send[...] = (xr[0].astype(F32) + xr[1].astype(F32)).astype(BF16).reshape(NZ, 48, SLICE)
    for d in range(1, NZ):
        to = (z + d) % NZ
        send(z_send.at[to], zr.at[z], z_ss.at[d - 1], z_rs.at[z], at(xl, to, y, h, r))
    total = z_send[z].astype(F32)
    for d in range(1, NZ):
        slot = (z + d) % NZ
        arrived(zr.at[slot], z_rs.at[slot])
        total = total + zr[slot].astype(F32)
    for k in range(8):
        f_send[k, 0:6, :] = total[6 * k : 6 * k + 6, :]
        f_send[k, 6:8, :] = jnp.zeros((2, SLICE), F32)
    f_recv[h, y] = f_send[mine]
    for d in range(NY):
        to = (y + d) % NY
        for c in range(2):
            if d == 0 and c == 0:
                continue
            core = (h + c) % 2
            send(
                f_send.at[2 * to + core], f_recv.at[h, y], f_ss.at[2 * d + c], f_rs.at[h, y],
                at(xl, z, to, core, r),
            )
    for d in range(NY):
        for c in range(2):
            if d == 0 and c == 0:
                continue
            core, frm = (h + c) % 2, (y + d) % NY
            arrived(f_recv.at[core, frm], f_rs.at[core, frm])
    for k in range(NY):
        cols = pl.ds(k * SLICE, SLICE)
        gwi_ref[:, cols] = f_recv[0, k, 0:6, :]
        gwt_ref[:, cols] = f_recv[1, k, 0:6, :]
    for finish in pending:
        finish()


def hand_over(*refs):
    for i in range(4):
        refs[4 + i][...] = refs[i][...]


def local(image_in, text_in, image_w, text_w, logit_scale, logit_bias):
    hbm = pl.BlockSpec(memory_space=pltpu.HBM)
    vmem = pl.BlockSpec(memory_space=pltpu.VMEM)
    smem = pl.BlockSpec(memory_space=pltpu.SMEM)
    dma = pltpu.SemaphoreType.DMA
    results = pl.pallas_call(
        body,
        name="contrast",
        out_shape=(
            jax.ShapeDtypeStruct((ROWS, HALF), BF16),
            jax.ShapeDtypeStruct((ROWS, HALF), BF16),
            jax.ShapeDtypeStruct((6, E), F32),
            jax.ShapeDtypeStruct((6, E), F32),
        ),
        in_specs=[hbm] * 4 + [smem] * 2,
        out_specs=(vmem,) * 4,
        scratch_shapes=[
            pltpu.VMEM((2, ROWS, HALF), BF16),
            pltpu.VMEM((2, HALF, E), BF16),
            pltpu.VMEM((2, ROWS, E), F32),
            pltpu.VMEM((2, ROWS, E), BF16),
            pltpu.VMEM((2, ROWS, E), BF16),
            pltpu.VMEM((SLOTS * ROWS, E), BF16),
            pltpu.VMEM((2, ROWS, E), BF16),
            pltpu.VMEM((ROWS, E), F32),
            pltpu.VMEM((ROWS, 1), F32),
            pltpu.VMEM((2, ROWS, SLOTS * ROWS), BF16),
            pltpu.VMEM((2, ROWS, E), F32),
            pltpu.VMEM((ROWS, E), F32),
            pltpu.VMEM((ROWS, E), BF16),
            pltpu.VMEM((NY, ROWS, SLICE), BF16),
            pltpu.VMEM((ROWS, E), BF16),
            pltpu.VMEM((2, ROWS, HALF), BF16),
            pltpu.VMEM((8, ROWS, HALF), BF16),
            pltpu.VMEM((8, ROWS, SLICE), BF16),
            pltpu.VMEM((2, HALF // 2, SLICE), BF16),
            pltpu.VMEM((2, HALF // 2, SLICE), BF16),
            pltpu.VMEM((NZ, 48, SLICE), BF16),
            pltpu.VMEM((NZ, 48, SLICE), BF16),
            pltpu.VMEM((8, 8, SLICE), F32),
            pltpu.VMEM((2, NY, 8, SLICE), F32),
            dma((4,)),
            dma((11,)),
            dma((8,)),
            dma((2, NCH)),
            dma((2, NCH)),
            dma((3, NCH)),
            dma((3, 3, NCH)),
            dma((SLOTS, NCH)),
            dma, dma,
            dma, dma,
            dma, dma,
            dma((7,)),
            dma((8,)),
            dma((2,)),
            dma((2,)),
            dma((7,)),
            dma((8,)),
            dma((8,)),
            dma((2, NY)),
        ],
        compiler_params=pltpu.CompilerParams(
            collective_id=0, has_side_effects=True, vmem_limit_bytes=60 << 20
        ),
    )(image_in, text_in, image_w, text_w, logit_scale.reshape(1, 1), logit_bias.reshape(1, 1))
    return pl.pallas_call(
        hand_over,
        name="hand_over",
        out_shape=tuple(jax.ShapeDtypeStruct(q.shape, q.dtype) for q in results),
        in_specs=[vmem] * 4,
        out_specs=(vmem,) * 4,
    )(*results)


def solution(mesh):
    placed = (P("dp", "mp"), P("dp", "mp"), P("mp", None), P("mp", None), P(), P())
    return jax.shard_map(
        local,
        mesh=mesh,
        in_specs=placed,
        out_specs=(P("dp", "mp"), P("dp", "mp"), P(("mp", "dp"), None), P(("mp", "dp"), None)),
        check_vma=False,
    )
```
